256 devices in a mesh: seq: 32 (over x, y, core), blk: 8 (over z).
Axes of the slice: x: 4, y: 4, z: 8, core: 2. Of those that a mesh axis runs over, the one named last changes fastest.
Arguments:
- alphas: float32 [2, 2048, 32768], P(None, 'seq', 'blk'), may hold values from 0.05 to 1
- betas: float32 [2, 2048, 65536], P(None, 'seq', 'blk'), may hold values from 0.05 to 1
- token_ids: int32 [2, 2048], P(None, 'seq'), may hold values from 0 to 31
- emission: float32 [32, 65536], P(None, 'blk'), may hold values from 0.05 to 1
- left_blocks: float32 [64, 128, 512], P('blk'), may hold values from 0.000390625 to 0.00390625
- right_blocks: float32 [128, 64, 512], P('blk', 'seq'), may hold values from 0.003125 to 0.03125
Outputs:
- left_grad: float32 [64, 128, 512], P('blk', 'seq')
- right_grad: float32 [128, 64, 512], P('blk', 'seq')
The draws below stay inside these ranges and needn't reach their ends.
All inputs are finite; a program needn't handle non-finite values.
Results may differ from the reference program's by a relative error of at most 0.0001.
Values sent between devices are 32-bit elements; how exact they have to be, the bound alone decides.
No kernel may reach another device: no remote copies, remote signals or barrier semaphores. Data moves between devices by JAX's collectives and lax.ppermute only.
A program may use at most 128 MiB of HBM per device.

```python
import math
import jax
import jax.numpy as jnp
from jax import lax

BS = 512
NB = 512
IW = 64
KW = 128
SEQ_DEV = 64
UNIQ = 32
SIN = 32768
SW = 65536
SEQS = 2048
N_SEQ = 32


def plant(entries, rng, least, largest):
    dims = entries.shape
    place = [jax.random.randint(jax.random.fold_in(rng, axis), (), 0, dims[axis]) for axis in range(len(dims))]
    entries = entries.at[tuple(place)].set(least)
    longest = dims.index(max(dims))
    place[longest] = (place[longest] + 1) % dims[longest]
    return entries.at[tuple(place)].set(largest)


def shard_levels(stream_key, extent, pieces, smallest, high):
    level = 1.0
    for position, parts in pieces:
        steps = jax.random.uniform(jax.random.fold_in(jax.random.fold_in(stream_key, 6), position), (parts,), jnp.float32, smallest / len(pieces), high / len(pieces))
        level = level * jnp.repeat(jnp.exp(steps), extent[position] // parts).reshape((-1,) + (1,) * (len(extent) - 1 - position))
    return level


def setup_inputs(seed: int = 0) -> dict:
    arg_keys = jax.random.split(jax.random.key(seed), 7)
    alphas = jnp.clip(jnp.exp(math.log(1.0) - 2.9957323 * jax.random.uniform(arg_keys[0], (2, SEQS, SIN), jnp.float32) ** shard_levels(arg_keys[0], (2, SEQS, SIN), ((1, 32), (2, 8)), -0.2, 0.2)), 0.05, 1.0)
    betas = jnp.clip(jnp.exp(math.log(1.0) - 2.9957323 * jax.random.uniform(arg_keys[1], (2, SEQS, SW), jnp.float32) ** shard_levels(arg_keys[1], (2, SEQS, SW), ((1, 32), (2, 8)), -0.2, 0.2)), 0.05, 1.0)
    token_ids = plant(jax.random.randint(arg_keys[2], (2, SEQS), 0, UNIQ), jax.random.fold_in(arg_keys[2], 1), 0, UNIQ - 1).astype(jnp.int32)
    emission = jnp.clip(jnp.exp(math.log(1.0) - 2.9957323 * jax.random.uniform(arg_keys[3], (UNIQ, SW), jnp.float32) ** shard_levels(arg_keys[3], (UNIQ, SW), ((1, 8),), -0.2, 0.2)), 0.05, 1.0)
    left_blocks = jnp.clip(jnp.exp(math.log(0.00390625) - 2.3025851 * jax.random.uniform(arg_keys[4], (IW, KW, BS), jnp.float32) ** shard_levels(arg_keys[4], (IW, KW, BS), ((0, 8),), -0.2, 0.2)), 0.000390625, 0.00390625)
    right_blocks = jnp.clip(jnp.exp(math.log(0.03125) - 2.3025851 * jax.random.uniform(arg_keys[5], (KW, IW, NB), jnp.float32) ** shard_levels(arg_keys[5], (KW, IW, NB), ((0, 8), (1, 32)), -0.2, 0.2)), 0.003125, 0.03125)
    return {"alphas": alphas, "betas": betas, "token_ids": token_ids, "emission": emission, "left_blocks": left_blocks, "right_blocks": right_blocks}


def reference(alphas, betas, token_ids, emission, left_blocks, right_blocks):
    seqs = alphas.shape[1]
    scale = (KW * NB) / (2.0 * seqs)
    count = 2 * N_SEQ
    alpha_blocks = alphas.reshape(count, SEQ_DEV, IW * BS)
    beta_blocks = betas.reshape(count, SEQ_DEV, KW * NB)
    id_blocks = token_ids.reshape(count, SEQ_DEV)
    high = lax.Precision.HIGHEST

    def visit(carry, item):
        grad_left, grad_right = carry
        a_flat, b_flat, ids = item
        a_rows = a_flat.reshape(SEQ_DEV, IW, BS)
        mixed = jnp.einsum('bij,ikj->bik', a_rows, left_blocks, precision=high)
        outputs = jnp.einsum('bik,kim->bkm', mixed, right_blocks, precision=high)
        rows = jnp.take(emission, ids, axis=0)
        signal = (rows * b_flat).reshape(SEQ_DEV, KW, NB)
        total = jnp.sum(outputs * signal, axis=(1, 2))
        weighted = signal * (scale / total)[:, None, None]
        grad_right = grad_right + jnp.einsum('bik,bkm->kim', mixed, weighted, precision=high)
        back = jnp.einsum('kim,bkm->bik', right_blocks, weighted, precision=high)
        grad_left = grad_left + jnp.einsum('bij,bik->ikj', a_rows, back, precision=high)
        return (grad_left, grad_right), None

    start = (jnp.zeros((IW, KW, BS), jnp.float32), jnp.zeros((KW, IW, NB), jnp.float32))
    (grad_left, grad_right), _ = lax.scan(visit, start, (alpha_blocks, beta_blocks, id_blocks))
    return grad_left, grad_right
```

```python
import functools

import jax
import jax.numpy as jnp
from jax import lax
from jax.experimental import pallas as pl
from jax.experimental.pallas import tpu as pltpu
from jax.sharding import Mesh, PartitionSpec as P

F32 = jnp.float32
BF16 = jnp.bfloat16
NT = (((1,), (1,)), ((), ()))
NN = (((1,), (0,)), ((), ()))
TN = (((0,), (0,)), ((), ()))
LANES = 128
MIB = 1024 * 1024
ANYWHERE = pl.BlockSpec(memory_space=pl.ANY)


def split(value):
    high = value.astype(BF16)
    low = (value - high.astype(F32)).astype(BF16)
    return high, low


def start(source, target, sem):
    copy = pltpu.make_async_copy(source, target, sem)
    copy.start()
    return copy


def dot3(a, b, dims):
    (ah, al), (bh, bl) = split(a), split(b)
    part = functools.partial(lax.dot_general, dimension_numbers=dims, preferred_element_type=F32)
    rows = a.shape[0]
    both = part(jnp.concatenate([ah, al], axis=0), bh)
    return both[:rows] + (part(ah, bl) + both[rows:])


def signal_kernel(tok_ref, emission_ref, betas_ref, g_ref, table_ref, held_ref, in_sem, out_sem):
    uniq, states = emission_ref.shape
    rows = betas_ref.shape[0]
    pieces = out_sem.shape[0]
    width = states // pieces
    waits = []
    for piece in range(pieces):
        columns = pl.ds(piece * width, width)
        waits.append(
            (
                start(emission_ref.at[:, columns], table_ref.at[:, columns], in_sem.at[0, piece]),
                start(betas_ref.at[:, columns], held_ref.at[:, columns], in_sem.at[1, piece]),
            )
        )
    tokens = jnp.concatenate([tok_ref[t : t + 1, :] for t in range(tok_ref.shape[0])], axis=1)
    pick = (lax.broadcasted_iota(jnp.int32, (uniq, rows), 0) == tokens).astype(F32).astype(BF16)
    pick = jnp.concatenate([pick, pick, pick], axis=0)
    outs = []
    for piece in range(pieces):
        columns = pl.ds(piece * width, width)
        for copy in waits[piece]:
            copy.wait()
        table = table_ref[:, columns]
        high, rest = split(table)
        middle, low = split(table - high.astype(F32))
        picked = lax.dot_general(
            pick, jnp.concatenate([high, middle, low], axis=0), TN, preferred_element_type=F32
        )
        held_ref[:, columns] = picked * held_ref[:, columns]
        outs.append(start(held_ref.at[:, columns], g_ref.at[:, columns], out_sem.at[piece]))
    for copy in outs:
        copy.wait()


def signal(tokens, emission, betas):
    pieces = 8
    return pl.pallas_call(
        signal_kernel,
        in_specs=[pl.BlockSpec(memory_space=pltpu.VMEM), ANYWHERE, ANYWHERE],
        out_specs=ANYWHERE,
        out_shape=jax.ShapeDtypeStruct(betas.shape, F32),
        scratch_shapes=[
            pltpu.VMEM(emission.shape, F32),
            pltpu.VMEM(betas.shape, F32),
            pltpu.SemaphoreType.DMA((2, pieces)),
            pltpu.SemaphoreType.DMA((pieces,)),
        ],
        compiler_params=pltpu.CompilerParams(vmem_limit_bytes=16 * MIB),
        name="signal",
    )(tokens, emission, betas)


def block_of(core, s):
    return 4 * (s // 2) + 2 * core + s % 2


def fetch_rows(core_ref, own_ref, other_ref, rows_ref, sem, mine):
    rows, width = own_ref.shape[0], rows_ref.shape[2]
    waits = []
    for s in range(mine):
        columns = pl.ds(pl.multiple_of(block_of(core_ref[0], s) * width, width), width)
        waits.append(
            [
                start(own_ref.at[:, columns], rows_ref.at[s, pl.ds(0, rows)], sem.at[0, s]),
                start(other_ref.at[:, columns], rows_ref.at[s, pl.ds(rows, rows)], sem.at[1, s]),
            ]
        )
    return waits


def mixed_kernel(core_ref, own_ref, other_ref, left_ref, u_ref, rows_ref, block_ref, sem, left_sem):
    mine = rows_ref.shape[0]
    waits = fetch_rows(core_ref, own_ref, other_ref, rows_ref, sem, mine)
    for s in range(mine):
        waits[s].append(start(left_ref.at[block_of(core_ref[0], s)], block_ref.at[s], left_sem.at[s]))
    zs, height, lanes = u_ref.shape
    band = height // mine
    part = band // 2
    for s in range(mine):
        for copy in waits[s]:
            copy.wait()
        u = dot3(block_ref[s], rows_ref[s], NT)
        for z in range(zs):
            for half in range(2):
                u_ref[z, s * band + half * part : s * band + (half + 1) * part, :] = u[
                    z * part : (z + 1) * part, half * lanes : (half + 1) * lanes
                ]


def mixed(core, own, other, left, zs):
    rows = own.shape[0]
    blocks, window, width = left.shape
    mine = blocks // 2
    return pl.pallas_call(
        mixed_kernel,
        in_specs=[pl.BlockSpec(memory_space=pltpu.SMEM), ANYWHERE, ANYWHERE, ANYWHERE],
        out_specs=pl.BlockSpec(memory_space=pltpu.VMEM),
        out_shape=jax.ShapeDtypeStruct((zs, mine * 2 * window // zs, rows), F32),
        scratch_shapes=[
            pltpu.VMEM((mine, 2 * rows, width), F32),
            pltpu.VMEM((mine, window, width), F32),
            pltpu.SemaphoreType.DMA((2, mine)),
            pltpu.SemaphoreType.DMA((mine,)),
        ],
        compiler_params=pltpu.CompilerParams(vmem_limit_bytes=8 * MIB),
        name="mixed",
    )(core, own, other, left)


def fetch_signal(own_ref, other_ref, g_ref, sem):
    rows, states = own_ref.shape
    pieces = sem.shape[1]
    width = states // pieces
    waits = []
    for piece in range(pieces):
        columns = pl.ds(piece * width, width)
        waits.append(
            (
                start(own_ref.at[:, columns], g_ref.at[pl.ds(0, rows), columns], sem.at[0, piece]),
                start(other_ref.at[:, columns], g_ref.at[pl.ds(rows, rows), columns], sem.at[1, piece]),
            )
        )
    return waits


def back_kernel(kcount, ways, place_ref, *refs):
    right_refs, refs = refs[: len(ways[0])], refs[len(ways[0]) :]
    own_ref, other_ref, u_ref, h_ref, g_ref, right_ref, held_ref, sem = refs
    waits = fetch_signal(own_ref, other_ref, g_ref, sem)
    lanes = u_ref.shape[1]
    nx, ny = len(ways[0]), len(ways[1])
    chips = nx * ny
    width = g_ref.shape[1] // kcount
    pieces = width // lanes
    krows = 2 * kcount * 2
    rrows = right_ref.shape[0] // chips
    for a, dx in enumerate(ways[0]):
        for b, dy in enumerate(ways[1]):
            x = lax.rem(place_ref[0] + (nx - dx), nx)
            y = lax.rem(place_ref[1] + (ny - dy), ny)
            chip = pl.multiple_of((x * ny + y) * rrows, rrows)
            right_ref[pl.ds(chip, rrows), :] = right_refs[a][b * rrows : (b + 1) * rrows, :]

    per_wait = kcount // len(waits)
    totals = [jnp.zeros((8, lanes), F32), jnp.zeros((8, lanes), F32)]
    for k in range(kcount):
        if k % per_wait == 0:
            for copy in waits[k // per_wait]:
                copy.wait()
        r = jnp.concatenate(
            [
                jnp.concatenate(
                    [
                        right_ref[pl.ds(k * 2 * pieces + 2 * piece + e, chips, stride=rrows), :]
                        for piece in range(pieces)
                    ],
                    axis=1,
                )
                for e in range(2)
            ],
            axis=0,
        )
        h = dot3(r, g_ref[:, k * width : (k + 1) * width], NT)
        for e in range(2):
            for half in range(2):
                place = pl.ds(e * 2 * kcount + half * kcount + k, chips, stride=krows)
                mine = h[e * chips : (e + 1) * chips, half * lanes : (half + 1) * lanes]
                held_ref[place, :] = mine
                both = u_ref[place, :] * mine
                for top in range(0, chips, 8):
                    totals[half] = totals[half] + both[top : top + 8, :]
    zs, height, _ = h_ref.shape
    body = height - 8
    own = jnp.sum(totals[0], axis=0, keepdims=True)
    other = jnp.sum(totals[1], axis=0, keepdims=True)
    line = lax.broadcasted_iota(jnp.int32, (8, lanes), 0)
    sums = jnp.where(line == 0, own, jnp.where(line == 1, other, 0.0))
    for z in range(zs):
        h_ref[z, 0:body, :] = held_ref[z * body : (z + 1) * body, :]
        h_ref[z, body:height, :] = sums


def back(place, ways, rights, own, other, u, zs, kcount):
    rows, states = own.shape
    pieces = 4
    body = u.shape[0] // zs
    whole = pl.BlockSpec(memory_space=pltpu.VMEM)
    right = (rights[0].shape[0] * len(rights), rights[0].shape[1])
    return pl.pallas_call(
        functools.partial(back_kernel, kcount, ways),
        in_specs=[
            pl.BlockSpec(memory_space=pltpu.SMEM),
            *[whole for _ in rights],
            ANYWHERE,
            ANYWHERE,
            whole,
        ],
        out_specs=whole,
        out_shape=jax.ShapeDtypeStruct((zs, body + 8, rows), F32),
        scratch_shapes=[
            pltpu.VMEM((2 * rows, states), F32),
            pltpu.VMEM(right, F32),
            pltpu.VMEM(u.shape, F32),
            pltpu.SemaphoreType.DMA((2, pieces)),
        ],
        compiler_params=pltpu.CompilerParams(vmem_limit_bytes=20 * MIB),
        name="back",
    )(place, *rights, own, other, u)


def weights_of(scale, mine, theirs):
    return [scale / (mine[row : row + 1, :] + theirs[1 - row : 2 - row, :]) for row in range(2)]


def right_kernel(kcount, chips, scale, u_ref, mine_ref, theirs_ref, own_ref, other_ref, out_ref, g_ref, sem):
    waits = fetch_signal(own_ref, other_ref, g_ref, sem)
    lanes = u_ref.shape[1]
    width = g_ref.shape[1] // kcount
    pieces = width // lanes
    krows = 2 * kcount * 2
    rrows = out_ref.shape[0] // chips
    weights = weights_of(scale, mine_ref[...], theirs_ref[...])
    per_wait = kcount // len(waits)
    for k in range(kcount):
        if k % per_wait == 0:
            for copy in waits[k // per_wait]:
                copy.wait()
        u = jnp.concatenate(
            [
                jnp.concatenate(
                    [
                        u_ref[pl.ds(e * 2 * kcount + half * kcount + k, chips, stride=krows), :] * weights[half]
                        for half in range(2)
                    ],
                    axis=1,
                )
                for e in range(2)
            ],
            axis=0,
        )
        grad = dot3(u, g_ref[:, k * width : (k + 1) * width], NN)
        for e in range(2):
            for piece in range(pieces):
                out_ref[pl.ds(k * 2 * pieces + 2 * piece + e, chips, stride=rrows), :] = grad[
                    e * chips : (e + 1) * chips, piece * lanes : (piece + 1) * lanes
                ]


def right_gradient(u, mine, theirs, own, other, chips, kcount, scale):
    rows, states = own.shape
    pieces = 4
    out = (chips * kcount * 2 * (states // kcount) // LANES, LANES)
    whole = pl.BlockSpec(memory_space=pltpu.VMEM)
    return pl.pallas_call(
        functools.partial(right_kernel, kcount, chips, scale),
        in_specs=[whole, whole, whole, ANYWHERE, ANYWHERE],
        out_specs=whole,
        out_shape=pltpu.HBM(out, F32),
        scratch_shapes=[pltpu.VMEM((2 * rows, states), F32), pltpu.SemaphoreType.DMA((2, pieces))],
        compiler_params=pltpu.CompilerParams(vmem_limit_bytes=20 * MIB),
        name="right_gradient",
    )(u, mine, theirs, own, other)


def left_kernel(chips, scale, core_ref, h_ref, mine_ref, theirs_ref, own_ref, other_ref, out_ref, rows_ref, sem):
    mine = rows_ref.shape[0]
    waits = fetch_rows(core_ref, own_ref, other_ref, rows_ref, sem, mine)
    zs, height, lanes = h_ref.shape
    per = (height - 8) // mine
    part = per // 2
    weights = weights_of(scale, mine_ref[...], theirs_ref[...])
    half_rows = out_ref.shape[1] // 2
    for s in range(mine):
        h = jnp.concatenate(
            [
                jnp.concatenate(
                    [h_ref[z, s * per + half * part : s * per + (half + 1) * part, :] for z in range(zs)], axis=0
                )
                * weights[half]
                for half in range(2)
            ],
            axis=1,
        )
        for copy in waits[s]:
            copy.wait()
        grad = dot3(h, rows_ref[s], NN)
        depth = grad.shape[0] // chips
        half_depth = depth // 2
        pieces = grad.shape[1] // lanes
        band = half_depth * pieces
        for chip in range(chips):
            for piece in range(pieces):
                tile = grad[chip * depth : (chip + 1) * depth, piece * lanes : (piece + 1) * lanes]
                for side in range(2):
                    first = side * half_rows + s * band + piece * half_depth
                    out_ref[chip, first : first + half_depth, :] = tile[side * half_depth : (side + 1) * half_depth, :]


def left_gradient(core, h, c_mine, c_theirs, own, other, chips, window, mine, scale):
    rows = own.shape[0]
    width = other.shape[1] // (2 * mine)
    out = (chips, mine * window * width // chips // LANES, LANES)
    whole = pl.BlockSpec(memory_space=pltpu.VMEM)
    return pl.pallas_call(
        functools.partial(left_kernel, chips, scale),
        in_specs=[pl.BlockSpec(memory_space=pltpu.SMEM), whole, whole, whole, ANYWHERE, ANYWHERE],
        out_specs=whole,
        out_shape=pltpu.HBM(out, F32),
        scratch_shapes=[pltpu.VMEM((mine, 2 * rows, width), F32), pltpu.SemaphoreType.DMA((2, mine))],
        compiler_params=pltpu.CompilerParams(vmem_limit_bytes=8 * MIB),
        name="left_gradient",
    )(core, h, c_mine, c_theirs, own, other)


def turn(value, axis, distance):
    if distance == 0:
        return value
    n = lax.axis_size(axis)
    return lax.ppermute(value, axis, [(i, (i + distance) % n) for i in range(n)])


def local(alphas, betas, token_ids, emission, left_blocks, right_blocks):
    steps, seq_dev, states_in = alphas.shape
    states_out = betas.shape[2]
    rows = steps * seq_dev
    blocks, window, width = left_blocks.shape
    kcount, rows_right, nblocks = right_blocks.shape
    zs = lax.axis_size("z")
    chips = lax.axis_size("x") * lax.axis_size("y")
    mine = blocks // 2
    pieces = nblocks // LANES
    scale = window * nblocks / (2.0 * seq_dev * chips * 2)
    core = lax.axis_index("c")
    core_arr = core.astype(jnp.int32).reshape(1)
    swap = functools.partial(lax.ppermute, axis_name="c", perm=[(0, 1), (1, 0)])

    right_rows = right_blocks.reshape(kcount, rows_right, pieces, LANES).transpose(0, 2, 1, 3)
    right_rows = right_rows.reshape(kcount * pieces * rows_right, LANES)
    ways = tuple((0, 1, n - 1) + tuple(range(2, n - 1)) for n in (lax.axis_size("x"), lax.axis_size("y")))
    right_y = jnp.concatenate([turn(right_rows, "y", d) for d in ways[1]], axis=0)
    place = jnp.stack([lax.axis_index("x"), lax.axis_index("y")]).astype(jnp.int32)

    alphas = alphas.reshape(rows, states_in)
    alphas_other = swap(alphas)

    in_hbm = functools.partial(pltpu.with_memory_space_constraint, memory_space=pltpu.HBM)
    g_own = signal(token_ids, in_hbm(emission), in_hbm(betas.reshape(rows, states_out)))
    alphas_other, right_y, g_own = lax.optimization_barrier((alphas_other, right_y, g_own))
    g_other = swap(g_own)

    u = mixed(core_arr, in_hbm(alphas), alphas_other, in_hbm(left_blocks), zs)
    u = lax.all_to_all(u, "z", split_axis=0, concat_axis=0, tiled=True).reshape(-1, rows)

    rights = [turn(right_y, "x", d) for d in ways[0]]
    h = back(place, ways, rights, g_own, g_other, u, zs, kcount)
    h = lax.all_to_all(h, "z", split_axis=0, concat_axis=0, tiled=True)
    c_mine = jnp.sum(h[:, -8:, :], axis=0)
    c_theirs = swap(c_mine)

    left_part = left_gradient(core_arr, h, c_mine, c_theirs, in_hbm(alphas), alphas_other, chips, window, mine, scale)
    left_parts = lax.all_to_all(left_part, ("x", "y"), split_axis=0, concat_axis=0, tiled=True)
    right_part = right_gradient(u, c_mine, c_theirs, g_own, g_other, chips, kcount, scale)
    right_part = right_part.reshape(chips, -1, LANES)
    right_parts = lax.all_to_all(right_part, ("x", "y"), split_axis=0, concat_axis=0, tiled=True)

    right_grad = jnp.sum(right_parts, axis=0).reshape(kcount, pieces, rows_right, LANES)
    right_grad = right_grad.transpose(0, 2, 1, 3).reshape(kcount, rows_right, nblocks)

    left_sum = jnp.sum(left_parts, axis=0)
    half = left_sum.shape[0] // 2
    sides = left_sum.reshape(2, half, LANES)
    keep = lax.dynamic_index_in_dim(sides, core, axis=0, keepdims=False)
    got = swap(lax.dynamic_index_in_dim(sides, 1 - core, axis=0, keepdims=False))
    depth = window // chips // 2
    shape = (blocks // 4, 2, pieces, depth, LANES)
    keep, got = keep.reshape(shape), got.reshape(shape)
    left_grad = jnp.where(core == 0, jnp.stack([keep, got], axis=1), jnp.stack([got, keep], axis=1))
    left_grad = left_grad.reshape(blocks, pieces, depth, LANES).transpose(0, 2, 1, 3)
    left_grad = left_grad.reshape(blocks, depth, width)
    return left_grad, right_grad


def solution(mesh):
    seq, blk = mesh.shape["seq"], mesh.shape["blk"]
    side = round((seq // 2) ** 0.5)
    fine = Mesh(mesh.devices.reshape(side, seq // 2 // side, 2, blk), ("x", "y", "c", "z"))
    s = ("x", "y", "c")
    placed = (
        P(None, s, "z"),
        P(None, s, "z"),
        P(None, s),
        P(None, "z"),
        P("z", None, None),
        P("z", s, None),
    )
    return jax.shard_map(
        local,
        mesh=fine,
        in_specs=placed,
        out_specs=(P("z", s, None), P("z", s, None)),
        check_vma=False,
    )
```

```python
import functools

import jax
import jax.numpy as jnp
from jax import lax
from jax.experimental import pallas as pl
from jax.experimental.pallas import tpu as pltpu
from jax.sharding import Mesh, PartitionSpec as P

F32 = jnp.float32
BF16 = jnp.bfloat16
NT = (((1,), (1,)), ((), ()))
NN = (((1,), (0,)), ((), ()))
TN = (((0,), (0,)), ((), ()))
LANES = 128
MIB = 1024 * 1024
ANYWHERE = pl.BlockSpec(memory_space=pl.ANY)
WHOLE = pl.BlockSpec(memory_space=pltpu.VMEM)
SCALARS = pl.BlockSpec(memory_space=pltpu.SMEM)


def split(value):
    high = value.astype(BF16)
    low = (value - high.astype(F32)).astype(BF16)
    return high, low


def start(source, target, sem):
    copy = pltpu.make_async_copy(source, target, sem)
    copy.start()
    return copy


def dot3(a, b, dims):
    (ah, al), (bh, bl) = split(a), split(b)
    part = functools.partial(lax.dot_general, dimension_numbers=dims, preferred_element_type=F32)
    rows = a.shape[0]
    both = part(jnp.concatenate([ah, al], axis=0), bh)
    return both[:rows] + (part(ah, bl) + both[rows:])


def signal_kernel(tok_ref, emission_ref, betas_ref, g_ref, table_ref, held_ref, in_sem, out_sem):
    uniq, states = emission_ref.shape
    rows = betas_ref.shape[0]
    pieces = out_sem.shape[0]
    width = states // pieces
    waits = []
    for piece in range(pieces):
        columns = pl.ds(piece * width, width)
        waits.append(
            (
                start(emission_ref.at[:, columns], table_ref.at[:, columns], in_sem.at[0, piece]),
                start(betas_ref.at[:, columns], held_ref.at[:, columns], in_sem.at[1, piece]),
            )
        )
    tokens = jnp.concatenate([tok_ref[t : t + 1, :] for t in range(tok_ref.shape[0])], axis=1)
    pick = (lax.broadcasted_iota(jnp.int32, (uniq, rows), 0) == tokens).astype(F32).astype(BF16)
    pick = jnp.concatenate([pick, pick, pick], axis=0)
    outs = []
    for piece in range(pieces):
        columns = pl.ds(piece * width, width)
        for copy in waits[piece]:
            copy.wait()
        table = table_ref[:, columns]
        high, rest = split(table)
        middle, low = split(table - high.astype(F32))
        picked = lax.dot_general(
            pick, jnp.concatenate([high, middle, low], axis=0), TN, preferred_element_type=F32
        )
        held_ref[:, columns] = picked * held_ref[:, columns]
        outs.append(start(held_ref.at[:, columns], g_ref.at[:, columns], out_sem.at[piece]))
    for copy in outs:
        copy.wait()


def signal(tokens, emission, betas):
    pieces = 8
    return pl.pallas_call(
        signal_kernel,
        in_specs=[pl.BlockSpec(memory_space=pltpu.VMEM), ANYWHERE, ANYWHERE],
        out_specs=ANYWHERE,
        out_shape=pltpu.HBM(betas.shape, F32),
        scratch_shapes=[
            pltpu.VMEM(emission.shape, F32),
            pltpu.VMEM(betas.shape, F32),
            pltpu.SemaphoreType.DMA((2, pieces)),
            pltpu.SemaphoreType.DMA((pieces,)),
        ],
        compiler_params=pltpu.CompilerParams(vmem_limit_bytes=16 * MIB),
        name="signal",
    )(tokens, emission, betas)


def mixed_kernel(rows_hbm, left_hbm, u_ref, rows_ref, left_ref, sem):
    blocks, _, width = left_ref.shape
    waits = []
    for i in range(blocks):
        columns = pl.ds(i * width, width)
        waits.append(
            (
                start(rows_hbm.at[:, columns], rows_ref.at[i], sem.at[0, i]),
                start(left_hbm.at[i], left_ref.at[i], sem.at[1, i]),
            )
        )
    zs, height, _ = u_ref.shape
    part = height // blocks
    for i in range(blocks):
        for copy in waits[i]:
            copy.wait()
        u = dot3(left_ref[i], rows_ref[i], NT)
        for z in range(zs):
            u_ref[z, i * part : (i + 1) * part, :] = u[z * part : (z + 1) * part]


def mixed(alphas, left, zs):
    rows = alphas.shape[0]
    blocks, window, width = left.shape
    return pl.pallas_call(
        mixed_kernel,
        in_specs=[ANYWHERE, ANYWHERE],
        out_specs=WHOLE,
        out_shape=jax.ShapeDtypeStruct((zs, blocks * window // zs, rows), F32),
        scratch_shapes=[
            pltpu.VMEM((blocks, rows, width), F32),
            pltpu.VMEM(left.shape, F32),
            pltpu.SemaphoreType.DMA((2, blocks)),
        ],
        compiler_params=pltpu.CompilerParams(vmem_limit_bytes=8 * MIB),
        name="mixed",
    )(alphas, left)


def place_of(k):
    return (k // 4 % 2) * 8 + k // 8 * 4 + k % 4


def back_kernel(kcount, ways, place_ref, *refs):
    slots = len(ways[0])
    rights, refs = (refs[:slots], refs[slots : 2 * slots]), refs[2 * slots :]
    signal_ref, u_ref, h_ref, send_ref, g_ref, right_ref, held_ref, sem = refs
    lanes = u_ref.shape[1]
    steps = sem.shape[0]
    share = g_ref.shape[1] // steps
    waits = []
    for step in range(steps):
        columns = pl.ds(step * share, share)
        waits.append(start(signal_ref.at[:, columns], g_ref.at[:, columns], sem.at[step]))
    nx, ny = slots, len(ways[1])
    chips = nx * ny
    width = g_ref.shape[1] // kcount
    pieces = width // lanes
    krows = 4 * kcount
    rrows = right_ref.shape[1] // chips
    core = place_ref[2]
    for side in range(2):
        owner = core if side == 0 else 1 - core
        for a, dx in enumerate(ways[0]):
            for b, dy in enumerate(ways[1]):
                x = lax.rem(place_ref[0] + (nx - dx), nx)
                y = lax.rem(place_ref[1] + (ny - dy), ny)
                chip = pl.multiple_of((x * ny + y) * rrows, rrows)
                right_ref[owner, pl.ds(chip, rrows), :] = rights[side][a][b * rrows : (b + 1) * rrows, :]

    part = 2 * kcount
    theirs = pl.multiple_of((1 - core) * part, part)
    for chip in range(chips):
        send_ref[chip * part : (chip + 1) * part, :] = u_ref[pl.ds(chip * 2 * part + theirs, part), :]

    total = jnp.zeros((8, lanes), F32)
    for k in range(kcount):
        if k * steps % kcount == 0:
            waits[k * steps // kcount].wait()
        r = jnp.concatenate(
            [
                jnp.concatenate(
                    [
                        right_ref[c, pl.ds(k * 2 * pieces + 2 * piece + e, chips, stride=rrows), :]
                        for piece in range(pieces)
                    ],
                    axis=1,
                )
                for c in range(2)
                for e in range(2)
            ],
            axis=0,
        )
        h = dot3(r, g_ref[:, k * width : (k + 1) * width], NT)
        for i in range(4):
            mine = h[i * chips : (i + 1) * chips, :]
            held_ref[pl.ds(i * kcount + place_of(k), chips, stride=krows), :] = mine
            both = u_ref[pl.ds(i * kcount + k, chips, stride=krows), :] * mine
            for top in range(0, chips, 8):
                total = total + both[top : top + 8, :]
    zs, height, _ = h_ref.shape
    body = height - 8
    total = jnp.broadcast_to(jnp.sum(total, axis=0, keepdims=True), total.shape)
    for z in range(zs):
        h_ref[z, 0:body, :] = held_ref[z * body : (z + 1) * body, :]
        h_ref[z, body:height, :] = total


def back(place, ways, rights, others, own, u, zs, kcount):
    rows, states = own.shape
    body = u.shape[0] // zs
    right = (2, rights[0].shape[0] * len(rights), rights[0].shape[1])
    return pl.pallas_call(
        functools.partial(back_kernel, kcount, ways),
        in_specs=[SCALARS, *[WHOLE for _ in (*rights, *others)], ANYWHERE, WHOLE],
        out_specs=(WHOLE, WHOLE),
        out_shape=(
            jax.ShapeDtypeStruct((zs, body + 8, rows), F32),
            jax.ShapeDtypeStruct((u.shape[0] // 2, rows), F32),
        ),
        scratch_shapes=[
            pltpu.VMEM((rows, states), F32),
            pltpu.VMEM(right, F32),
            pltpu.VMEM(u.shape, F32),
            pltpu.SemaphoreType.DMA((4,)),
        ],
        compiler_params=pltpu.CompilerParams(vmem_limit_bytes=16 * MIB),
        name="back",
    )(place, *rights, *others, own, u)


def pick_h_kernel(place_ref, h_ref, send_ref):
    zs, height, _ = h_ref.shape
    first = pl.multiple_of((1 - place_ref[2]) * 8, 8)
    total = h_ref[0, height - 8 : height, :]
    for z in range(1, zs):
        total = total + h_ref[z, height - 8 : height, :]
    bands = (height - 8) // 16
    for z in range(zs):
        for band in range(bands):
            send_ref[(z * bands + band) * 8 : (z * bands + band + 1) * 8, :] = h_ref[z, pl.ds(band * 16 + first, 8), :]
    send_ref[zs * bands * 8 :, :] = total


def pick_h(place, h):
    zs, height, lanes = h.shape
    return pl.pallas_call(
        pick_h_kernel,
        in_specs=[SCALARS, WHOLE],
        out_specs=WHOLE,
        out_shape=jax.ShapeDtypeStruct((zs * (height - 8) // 2 + 8, lanes), F32),
        compiler_params=pltpu.CompilerParams(vmem_limit_bytes=4 * MIB),
        name="pick_h",
    )(place, h)


def gradients_kernel(kcount, scale, place_ref, h_ref, sent_ref, got_ref, u_ref, uo_ref, *refs):
    rows_refs, g_refs, (out_ref, rows_ref, g_ref, rows_sem, g_sem) = refs[:2], refs[2:4], refs[4:]
    blocks, both, width = rows_ref.shape
    lanes = both // 2
    rows_waits, g_waits = [], []
    for i in range(blocks):
        columns = pl.ds(i * width, width)
        rows_waits.append(
            [start(rows_refs[n].at[:, columns], rows_ref.at[i, pl.ds(n * lanes, lanes)], rows_sem.at[n, i]) for n in range(2)]
        )
    steps = g_sem.shape[1]
    share = g_ref.shape[1] // steps
    for step in range(steps):
        columns = pl.ds(step * share, share)
        g_waits.append(
            [start(g_refs[n].at[:, columns], g_ref.at[pl.ds(n * lanes, lanes), columns], g_sem.at[n, step]) for n in range(2)]
        )
    core = place_ref[2]
    chips, out_rows, _ = out_ref.shape
    pieces = width // lanes
    zs = h_ref.shape[0]
    last = sent_ref.shape[0] - 8
    weights = [scale / sent_ref[last : last + 1, :], scale / got_ref[last : last + 1, :]]

    keep = pl.multiple_of(core * 8, 8)
    for i in range(blocks):
        own = jnp.concatenate([h_ref[z, pl.ds(i * 16 + keep, 8), :] for z in range(zs)], axis=0)
        other = jnp.concatenate([got_ref[(z * blocks + i) * 8 : (z * blocks + i + 1) * 8, :] for z in range(zs)], axis=0)
        h = jnp.concatenate([own * weights[0], other * weights[1]], axis=1)
        for copy in rows_waits[i]:
            copy.wait()
        grad = dot3(h, rows_ref[i], NN)
        depth = grad.shape[0] // chips
        for chip in range(chips):
            for piece in range(pieces):
                first = (i * pieces + piece) * depth
                out_ref[chip, first : first + depth, :] = grad[
                    chip * depth : (chip + 1) * depth, piece * lanes : (piece + 1) * lanes
                ]

    middle = out_rows // 2
    flat_ref = out_ref.reshape(chips * out_rows, lanes)
    g_width = g_ref.shape[1] // kcount
    g_pieces = g_width // lanes
    for k in range(kcount):
        if k * steps % kcount == 0:
            for copy in g_waits[k * steps // kcount]:
                copy.wait()
        u = jnp.concatenate(
            [
                jnp.concatenate(
                    [
                        u_ref[pl.ds((2 * core + e) * kcount + k, chips, stride=4 * kcount), :] * weights[0],
                        uo_ref[pl.ds(e * kcount + k, chips, stride=2 * kcount), :] * weights[1],
                    ],
                    axis=1,
                )
                for e in range(2)
            ],
            axis=0,
        )
        grad = dot3(u, g_ref[:, k * g_width : (k + 1) * g_width], NN)
        for e in range(2):
            for piece in range(g_pieces):
                place = pl.ds(middle + (k * g_pieces + piece) * 2 + e, chips, stride=out_rows)
                flat_ref[place, :] = grad[e * chips : (e + 1) * chips, piece * lanes : (piece + 1) * lanes]


def gradients(place, h, sent, got, u, u_other, alphas, g, chips, kcount, blocks, scale):
    rows, states_in = alphas[0].shape
    states = g[0].shape[1]
    out_rows = (blocks // 2 * (states_in // blocks) * kcount * h.shape[0] + 2 * states * chips) // LANES // chips
    steps = 4
    return pl.pallas_call(
        functools.partial(gradients_kernel, kcount, scale),
        in_specs=[SCALARS] + [WHOLE] * 5 + [ANYWHERE] * 4,
        out_specs=WHOLE,
        out_shape=jax.ShapeDtypeStruct((chips, out_rows, LANES), F32),
        scratch_shapes=[
            pltpu.VMEM((blocks, 2 * rows, states_in // blocks), F32),
            pltpu.VMEM((2 * rows, states), F32),
            pltpu.SemaphoreType.DMA((2, blocks)),
            pltpu.SemaphoreType.DMA((2, steps)),
        ],
        compiler_params=pltpu.CompilerParams(vmem_limit_bytes=16 * MIB),
        name="gradients",
    )(place, h, sent, got, u, u_other, *alphas, *g)


def turn(value, axis, distance):
    if distance == 0:
        return value
    n = lax.axis_size(axis)
    return lax.ppermute(value, axis, [(i, (i + distance) % n) for i in range(n)])


def local(alphas, betas, token_ids, emission, left_blocks, right_blocks):
    steps, seq_dev, states_in = alphas.shape
    states_out = betas.shape[2]
    rows = steps * seq_dev
    blocks, window, width = left_blocks.shape
    kcount, rows_right, nblocks = right_blocks.shape
    zs = lax.axis_size("z")
    chips = lax.axis_size("x") * lax.axis_size("y")
    pieces = nblocks // LANES
    scale = window * nblocks / (2.0 * seq_dev * chips * 2)
    swap = functools.partial(lax.ppermute, axis_name="c", perm=[(0, 1), (1, 0)])
    in_hbm = functools.partial(pltpu.with_memory_space_constraint, memory_space=pltpu.HBM)
    place = jnp.stack([lax.axis_index(name) for name in ("x", "y", "c")]).astype(jnp.int32)
    alphas = alphas.reshape(rows, states_in)
    betas = in_hbm(betas.reshape(rows, states_out))

    right_rows = right_blocks.reshape(kcount, rows_right, pieces, LANES).transpose(0, 2, 1, 3)
    right_rows = right_rows.reshape(kcount * pieces * rows_right, LANES)
    ways = tuple((0, 1, n - 1) + tuple(range(2, n - 1)) for n in (lax.axis_size("x"), lax.axis_size("y")))
    right_y = jnp.concatenate([turn(right_rows, "y", d) for d in ways[1]], axis=0)

    u = mixed(in_hbm(alphas), in_hbm(left_blocks), zs)
    u, right_y = lax.optimization_barrier((u, right_y))
    u = lax.all_to_all(u, "z", split_axis=0, concat_axis=0, tiled=True).reshape(-1, rows)
    rights = [turn(right_y, "x", d) for d in ways[0]]
    g_own = signal(token_ids, in_hbm(emission), betas)
    rights[1], g_own = lax.optimization_barrier((rights[1], g_own))
    others = [swap(part) for part in rights]

    h, u_sent = back(place, ways, rights, others, in_hbm(g_own), u, zs, kcount)
    h, g_later = lax.optimization_barrier((h, g_own))
    h = lax.all_to_all(h, "z", split_axis=0, concat_axis=0, tiled=True)
    sent = pick_h(place, h)
    got = swap(sent)

    u_other = swap(u_sent)
    two_alphas, two_g = (in_hbm(alphas), swap(alphas)), (in_hbm(g_later), swap(g_later))
    part = gradients(place, h, sent, got, u, u_other, two_alphas, two_g, chips, kcount, blocks, scale)
    parts = lax.all_to_all(part, ("x", "y"), split_axis=0, concat_axis=0, tiled=True)
    total = jnp.sum(parts, axis=0)
    middle = total.shape[0] // 2
    left_grad = total[:middle].reshape(blocks, pieces, -1, LANES).transpose(0, 2, 1, 3).reshape(blocks, -1, width)
    right_grad = total[middle:].reshape(kcount, pieces, rows_right, LANES).transpose(0, 2, 1, 3)
    return left_grad, right_grad.reshape(kcount, rows_right, nblocks)


def solution(mesh):
    seq, blk = mesh.shape["seq"], mesh.shape["blk"]
    side = round((seq // 2) ** 0.5)
    fine = Mesh(mesh.devices.reshape(side, seq // 2 // side, 2, blk), ("x", "y", "c", "z"))
    s = ("x", "y", "c")
    placed = (
        P(None, s, "z"),
        P(None, s, "z"),
        P(None, s),
        P(None, "z"),
        P("z", None, None),
        P("z", s, None),
    )
    return jax.shard_map(
        local,
        mesh=fine,
        in_specs=placed,
        out_specs=(P("z", s, None), P("z", s, None)),
        check_vma=False,
    )
```

```python
import functools

import jax
import jax.numpy as jnp
from jax import lax
from jax.experimental import pallas as pl
from jax.experimental.pallas import tpu as pltpu
from jax.sharding import Mesh, PartitionSpec as P

F32 = jnp.float32
BF16 = jnp.bfloat16
NT = (((1,), (1,)), ((), ()))
NN = (((1,), (0,)), ((), ()))
TN = (((0,), (0,)), ((), ()))
LANES = 128
MIB = 1024 * 1024
ANYWHERE = pl.BlockSpec(memory_space=pl.ANY)
WHOLE = pl.BlockSpec(memory_space=pltpu.VMEM)
SCALARS = pl.BlockSpec(memory_space=pltpu.SMEM)


def split(value):
    high = value.astype(BF16)
    low = (value - high.astype(F32)).astype(BF16)
    return high, low


def start(source, target, sem):
    copy = pltpu.make_async_copy(source, target, sem)
    copy.start()
    return copy


def dot3(a, b, dims):
    (ah, al), (bh, bl) = split(a), split(b)
    part = functools.partial(lax.dot_general, dimension_numbers=dims, preferred_element_type=F32)
    rows = a.shape[0]
    both = part(jnp.concatenate([ah, al], axis=0), bh)
    return both[:rows] + (part(ah, bl) + both[rows:])


def signal_kernel(tok_ref, emission_ref, betas_ref, g_ref, table_ref, held_ref, in_sem, out_sem):
    uniq, states = emission_ref.shape
    rows = betas_ref.shape[0]
    pieces = out_sem.shape[0]
    width = states // pieces
    waits = []
    for piece in range(pieces):
        columns = pl.ds(piece * width, width)
        waits.append(
            (
                start(emission_ref.at[:, columns], table_ref.at[:, columns], in_sem.at[0, piece]),
                start(betas_ref.at[:, columns], held_ref.at[:, columns], in_sem.at[1, piece]),
            )
        )
    tokens = jnp.concatenate([tok_ref[t : t + 1, :] for t in range(tok_ref.shape[0])], axis=1)
    pick = (lax.broadcasted_iota(jnp.int32, (uniq, rows), 0) == tokens).astype(F32).astype(BF16)
    pick = jnp.concatenate([pick, pick, pick], axis=0)
    outs = []
    for piece in range(pieces):
        columns = pl.ds(piece * width, width)
        for copy in waits[piece]:
            copy.wait()
        table = table_ref[:, columns]
        high, rest = split(table)
        middle, low = split(table - high.astype(F32))
        picked = lax.dot_general(
            pick, jnp.concatenate([high, middle, low], axis=0), TN, preferred_element_type=F32
        )
        held_ref[:, columns] = picked * held_ref[:, columns]
        outs.append(start(held_ref.at[:, columns], g_ref.at[:, columns], out_sem.at[piece]))
    for copy in outs:
        copy.wait()


def signal(tokens, emission, betas):
    pieces = 8
    return pl.pallas_call(
        signal_kernel,
        in_specs=[pl.BlockSpec(memory_space=pltpu.VMEM), ANYWHERE, ANYWHERE],
        out_specs=ANYWHERE,
        out_shape=pltpu.HBM(betas.shape, F32),
        scratch_shapes=[
            pltpu.VMEM(emission.shape, F32),
            pltpu.VMEM(betas.shape, F32),
            pltpu.SemaphoreType.DMA((2, pieces)),
            pltpu.SemaphoreType.DMA((pieces,)),
        ],
        compiler_params=pltpu.CompilerParams(vmem_limit_bytes=20 * MIB),
        name="signal",
    )(tokens, emission, betas)


def mixed_kernel(rows_hbm, left_hbm, u_ref, rows_ref, left_ref, sem):
    blocks, _, width = left_ref.shape
    waits = []
    for i in range(blocks):
        columns = pl.ds(i * width, width)
        waits.append(
            (
                start(rows_hbm.at[:, columns], rows_ref.at[i], sem.at[0, i]),
                start(left_hbm.at[i], left_ref.at[i], sem.at[1, i]),
            )
        )
    zs, height, _ = u_ref.shape
    part = height // blocks
    for i in range(blocks):
        for copy in waits[i]:
            copy.wait()
        u = dot3(left_ref[i], rows_ref[i], NT)
        for z in range(zs):
            u_ref[z, i * part : (i + 1) * part, :] = u[z * part : (z + 1) * part]


def mixed(alphas, left, zs):
    rows = alphas.shape[0]
    blocks, window, width = left.shape
    return pl.pallas_call(
        mixed_kernel,
        in_specs=[ANYWHERE, ANYWHERE],
        out_specs=WHOLE,
        out_shape=jax.ShapeDtypeStruct((zs, blocks * window // zs, rows), F32),
        scratch_shapes=[
            pltpu.VMEM((blocks, rows, width), F32),
            pltpu.VMEM(left.shape, F32),
            pltpu.SemaphoreType.DMA((2, blocks)),
        ],
        compiler_params=pltpu.CompilerParams(vmem_limit_bytes=8 * MIB),
        name="mixed",
    )(alphas, left)


def place_of(k):
    return (k // 4 % 2) * 8 + k // 8 * 4 + k % 4


def back_kernel(kcount, ways, place_ref, *refs):
    slots = len(ways)
    rights, refs = (refs[:slots], refs[slots : 2 * slots]), refs[2 * slots :]
    signal_ref, u_ref, h_ref, send_ref, g_ref, right_ref, held_ref, sem = refs
    lanes = u_ref.shape[1]
    steps = sem.shape[0]
    share = g_ref.shape[1] // steps
    waits = []
    for step in range(steps):
        columns = pl.ds(step * share, share)
        waits.append(start(signal_ref.at[:, columns], g_ref.at[:, columns], sem.at[step]))
    chips = slots * slots
    width = g_ref.shape[1] // kcount
    pieces = width // lanes
    krows = 4 * kcount
    rrows = right_ref.shape[1] // chips
    core = place_ref[2]
    for side in range(2):
        owner = core if side == 0 else 1 - core
        on_x = owner == 0
        late = jnp.where(on_x, place_ref[0], place_ref[1])
        early = jnp.where(on_x, place_ref[1], place_ref[0])
        for a, da in enumerate(ways):
            for b, db in enumerate(ways):
                first = lax.rem(late + (slots - da), slots)
                second = lax.rem(early + (slots - db), slots)
                x, y = jnp.where(on_x, first, second), jnp.where(on_x, second, first)
                chip = pl.multiple_of((x * slots + y) * rrows, rrows)
                right_ref[owner, pl.ds(chip, rrows), :] = rights[side][a][b * rrows : (b + 1) * rrows, :]

    part = 2 * kcount
    theirs = pl.multiple_of((1 - core) * part, part)
    for chip in range(chips):
        send_ref[chip * part : (chip + 1) * part, :] = u_ref[pl.ds(chip * 2 * part + theirs, part), :]

    total = jnp.zeros((8, lanes), F32)
    for k in range(kcount):
        if k * steps % kcount == 0:
            waits[k * steps // kcount].wait()
        r = jnp.concatenate(
            [
                jnp.concatenate(
                    [
                        right_ref[c, pl.ds(k * 2 * pieces + 2 * piece + e, chips, stride=rrows), :]
                        for piece in range(pieces)
                    ],
                    axis=1,
                )
                for c in range(2)
                for e in range(2)
            ],
            axis=0,
        )
        h = dot3(r, g_ref[:, k * width : (k + 1) * width], NT)
        for i in range(4):
            mine = h[i * chips : (i + 1) * chips, :]
            held_ref[pl.ds(i * kcount + place_of(k), chips, stride=krows), :] = mine
            both = u_ref[pl.ds(i * kcount + k, chips, stride=krows), :] * mine
            for top in range(0, chips, 8):
                total = total + both[top : top + 8, :]
    zs, height, _ = h_ref.shape
    body = height - 8
    total = jnp.broadcast_to(jnp.sum(total, axis=0, keepdims=True), total.shape)
    for z in range(zs):
        h_ref[z, 0:body, :] = held_ref[z * body : (z + 1) * body, :]
        h_ref[z, body:height, :] = total


def back(place, ways, rights, others, own, u, zs, kcount):
    rows, states = own.shape
    body = u.shape[0] // zs
    right = (2, rights[0].shape[0] * len(rights), rights[0].shape[1])
    return pl.pallas_call(
        functools.partial(back_kernel, kcount, ways),
        in_specs=[SCALARS, *[WHOLE for _ in (*rights, *others)], ANYWHERE, WHOLE],
        out_specs=(WHOLE, WHOLE),
        out_shape=(
            jax.ShapeDtypeStruct((zs, body + 8, rows), F32),
            jax.ShapeDtypeStruct((u.shape[0] // 2, rows), F32),
        ),
        scratch_shapes=[
            pltpu.VMEM((rows, states), F32),
            pltpu.VMEM(right, F32),
            pltpu.VMEM(u.shape, F32),
            pltpu.SemaphoreType.DMA((4,)),
        ],
        compiler_params=pltpu.CompilerParams(vmem_limit_bytes=20 * MIB),
        name="back",
    )(place, *rights, *others, own, u)


def pick_h_kernel(place_ref, h_ref, send_ref):
    zs, height, _ = h_ref.shape
    first = pl.multiple_of((1 - place_ref[2]) * 8, 8)
    total = h_ref[0, height - 8 : height, :]
    for z in range(1, zs):
        total = total + h_ref[z, height - 8 : height, :]
    bands = (height - 8) // 16
    for z in range(zs):
        for band in range(bands):
            send_ref[(z * bands + band) * 8 : (z * bands + band + 1) * 8, :] = h_ref[z, pl.ds(band * 16 + first, 8), :]
    send_ref[zs * bands * 8 :, :] = total


def pick_h(place, h):
    zs, height, lanes = h.shape
    return pl.pallas_call(
        pick_h_kernel,
        in_specs=[SCALARS, WHOLE],
        out_specs=WHOLE,
        out_shape=jax.ShapeDtypeStruct((zs * (height - 8) // 2 + 8, lanes), F32),
        compiler_params=pltpu.CompilerParams(vmem_limit_bytes=4 * MIB),
        name="pick_h",
    )(place, h)


def gradients_kernel(kcount, scale, place_ref, h_ref, sent_ref, got_ref, u_ref, uo_ref, *refs):
    rows_refs, g_refs, (out_ref, rows_ref, g_ref, held_ref, rows_sem, g_sem) = refs[:2], refs[2:4], refs[4:]
    blocks, both, width = rows_ref.shape
    lanes = both // 2
    rows_waits, g_waits = [], []
    for i in range(blocks):
        columns = pl.ds(i * width, width)
        rows_waits.append(
            [start(rows_refs[n].at[:, columns], rows_ref.at[i, pl.ds(n * lanes, lanes)], rows_sem.at[n, i]) for n in range(2)]
        )
    steps = g_sem.shape[1]
    share = g_ref.shape[1] // steps
    for step in range(steps):
        columns = pl.ds(step * share, share)
        g_waits.append(
            [start(g_refs[n].at[:, columns], g_ref.at[pl.ds(n * lanes, lanes), columns], g_sem.at[n, step]) for n in range(2)]
        )
    core = place_ref[2]
    chips, out_rows, _ = out_ref.shape
    pieces = width // lanes
    zs = h_ref.shape[0]
    last = sent_ref.shape[0] - 8
    weights = [scale / sent_ref[last : last + 1, :], scale / got_ref[last : last + 1, :]]

    side = round(chips**0.5)
    spots = [jnp.where(core == 0, chip, chip % side * side + chip // side) for chip in range(chips)]
    keep = pl.multiple_of(core * 8, 8)
    for i in range(blocks):
        own = jnp.concatenate([h_ref[z, pl.ds(i * 16 + keep, 8), :] for z in range(zs)], axis=0)
        other = jnp.concatenate([got_ref[(z * blocks + i) * 8 : (z * blocks + i + 1) * 8, :] for z in range(zs)], axis=0)
        h = jnp.concatenate([own * weights[0], other * weights[1]], axis=1)
        for copy in rows_waits[i]:
            copy.wait()
        grad = dot3(h, rows_ref[i], NN)
        depth = grad.shape[0] // chips
        for chip in range(chips):
            for piece in range(pieces):
                first = (i * pieces + piece) * depth
                out_ref[spots[chip], first : first + depth, :] = grad[
                    chip * depth : (chip + 1) * depth, piece * lanes : (piece + 1) * lanes
                ]

    middle = out_rows // 2
    g_width = g_ref.shape[1] // kcount
    g_pieces = g_width // lanes
    for k in range(kcount):
        if k * steps % kcount == 0:
            for copy in g_waits[k * steps // kcount]:
                copy.wait()
        u = jnp.concatenate(
            [
                jnp.concatenate(
                    [
                        u_ref[pl.ds((2 * core + e) * kcount + k, chips, stride=4 * kcount), :] * weights[0],
                        uo_ref[pl.ds(e * kcount + k, chips, stride=2 * kcount), :] * weights[1],
                    ],
                    axis=1,
                )
                for e in range(2)
            ],
            axis=0,
        )
        grad = dot3(u, g_ref[:, k * g_width : (k + 1) * g_width], NN)
        for e in range(2):
            for piece in range(g_pieces):
                place = pl.ds((k * g_pieces + piece) * 2 + e, chips, stride=middle)
                held_ref[place, :] = grad[e * chips : (e + 1) * chips, piece * lanes : (piece + 1) * lanes]
    for chip in range(chips):
        out_ref[spots[chip], middle:, :] = held_ref[chip * middle : (chip + 1) * middle, :]


def gradients(place, h, sent, got, u, u_other, alphas, g, chips, kcount, blocks, scale):
    rows, states_in = alphas[0].shape
    states = g[0].shape[1]
    out_rows = (blocks // 2 * (states_in // blocks) * kcount * h.shape[0] + 2 * states * chips) // LANES // chips
    steps = 4
    return pl.pallas_call(
        functools.partial(gradients_kernel, kcount, scale),
        in_specs=[SCALARS] + [WHOLE] * 5 + [ANYWHERE] * 4,
        out_specs=WHOLE,
        out_shape=jax.ShapeDtypeStruct((chips, out_rows, LANES), F32),
        scratch_shapes=[
            pltpu.VMEM((blocks, 2 * rows, states_in // blocks), F32),
            pltpu.VMEM((2 * rows, states), F32),
            pltpu.VMEM((chips * out_rows // 2, LANES), F32),
            pltpu.SemaphoreType.DMA((2, blocks)),
            pltpu.SemaphoreType.DMA((2, steps)),
        ],
        compiler_params=pltpu.CompilerParams(vmem_limit_bytes=20 * MIB),
        name="gradients",
    )(place, h, sent, got, u, u_other, *alphas, *g)


def along(stage, core):
    return (stage + core) % 2


def members(nx, ny, stage):
    index = lambda x, y, c: (x * ny + y) * 2 + c
    groups = []
    for c in range(2):
        if along(stage, c) == 0:
            groups += [[index(x, y, c) for x in range(nx)] for y in range(ny)]
        else:
            groups += [[index(x, y, c) for y in range(ny)] for x in range(nx)]
    return groups


def turn(value, groups, distance):
    if distance == 0:
        return value
    pairs = [(line[n], line[(n + distance) % len(line)]) for line in groups for n in range(len(line))]
    return lax.ppermute(value, ("x", "y", "c"), pairs)


def scatter(value, groups):
    parts = lax.all_to_all(
        value, ("x", "y", "c"), split_axis=0, concat_axis=0, axis_index_groups=groups, tiled=True
    )
    n = len(groups[0])
    return jnp.sum(parts.reshape(n, value.shape[0] // n, *value.shape[1:]), axis=0)


def local(alphas, betas, token_ids, emission, left_blocks, right_blocks):
    steps, seq_dev, states_in = alphas.shape
    states_out = betas.shape[2]
    rows = steps * seq_dev
    blocks, window, width = left_blocks.shape
    kcount, rows_right, nblocks = right_blocks.shape
    zs = lax.axis_size("z")
    chips = lax.axis_size("x") * lax.axis_size("y")
    pieces = nblocks // LANES
    scale = window * nblocks / (2.0 * seq_dev * chips * 2)
    swap = functools.partial(lax.ppermute, axis_name="c", perm=[(0, 1), (1, 0)])
    in_hbm = functools.partial(pltpu.with_memory_space_constraint, memory_space=pltpu.HBM)
    place = jnp.stack([lax.axis_index(name) for name in ("x", "y", "c")]).astype(jnp.int32)
    alphas = alphas.reshape(rows, states_in)
    betas = in_hbm(betas.reshape(rows, states_out))

    right_rows = right_blocks.reshape(kcount, rows_right, pieces, LANES).transpose(0, 2, 1, 3)
    right_rows = right_rows.reshape(kcount * pieces * rows_right, LANES)
    side = lax.axis_size("x")
    lines = [members(side, side, stage) for stage in range(2)]
    ways = (0, 1, side - 1) + tuple(range(2, side - 1))
    right_y = jnp.concatenate([turn(right_rows, lines[1], d) for d in ways], axis=0)

    u = mixed(in_hbm(alphas), in_hbm(left_blocks), zs)
    u, right_y = lax.optimization_barrier((u, right_y))
    u = lax.all_to_all(u, "z", split_axis=0, concat_axis=0, tiled=True).reshape(-1, rows)
    rights = [turn(right_y, lines[0], d) for d in ways]
    g_own = signal(token_ids, in_hbm(emission), betas)
    rights[1], g_own = lax.optimization_barrier((rights[1], g_own))
    others = [swap(part) for part in rights]

    h, u_sent = back(place, ways, rights, others, in_hbm(g_own), u, zs, kcount)
    h, g_later = lax.optimization_barrier((h, g_own))
    h = lax.all_to_all(h, "z", split_axis=0, concat_axis=0, tiled=True)
    sent = pick_h(place, h)
    got = swap(sent)

    u_other = swap(u_sent)
    two_alphas, two_g = (in_hbm(alphas), swap(alphas)), (in_hbm(g_later), swap(g_later))
    part = gradients(place, h, sent, got, u, u_other, two_alphas, two_g, chips, kcount, blocks, scale)
    total = scatter(scatter(part, lines[0]), lines[1])[0]
    middle = total.shape[0] // 2
    left_grad = total[:middle].reshape(blocks, pieces, -1, LANES).transpose(0, 2, 1, 3).reshape(blocks, -1, width)
    right_grad = total[middle:].reshape(kcount, pieces, rows_right, LANES).transpose(0, 2, 1, 3)
    return left_grad, right_grad.reshape(kcount, rows_right, nblocks)


def solution(mesh):
    seq, blk = mesh.shape["seq"], mesh.shape["blk"]
    side = round((seq // 2) ** 0.5)
    fine = Mesh(mesh.devices.reshape(side, seq // 2 // side, 2, blk), ("x", "y", "c", "z"))
    s = ("x", "y", "c")
    placed = (
        P(None, s, "z"),
        P(None, s, "z"),
        P(None, s),
        P(None, "z"),
        P("z", None, None),
        P("z", s, None),
    )
    return jax.shard_map(
        local,
        mesh=fine,
        in_specs=placed,
        out_specs=(P("z", s, None), P("z", s, None)),
        check_vma=False,
    )
```

```python
import functools

import jax
import jax.numpy as jnp
from jax import lax
from jax.experimental import pallas as pl
from jax.experimental.pallas import tpu as pltpu
from jax.sharding import Mesh, PartitionSpec as P

F32 = jnp.float32
BF16 = jnp.bfloat16
NT = (((1,), (1,)), ((), ()))
NN = (((1,), (0,)), ((), ()))
TN = (((0,), (0,)), ((), ()))
LANES = 128
MIB = 1024 * 1024
ANYWHERE = pl.BlockSpec(memory_space=pl.ANY)
WHOLE = pl.BlockSpec(memory_space=pltpu.VMEM)
SCALARS = pl.BlockSpec(memory_space=pltpu.SMEM)


def split(value):
    high = value.astype(BF16)
    low = (value - high.astype(F32)).astype(BF16)
    return high, low


def start(source, target, sem):
    copy = pltpu.make_async_copy(source, target, sem)
    copy.start()
    return copy


def dot3(a, b, dims):
    (ah, al), (bh, bl) = split(a), split(b)
    part = functools.partial(lax.dot_general, dimension_numbers=dims, preferred_element_type=F32)
    rows = a.shape[0]
    both = part(jnp.concatenate([ah, al], axis=0), bh)
    return both[:rows] + (part(ah, bl) + both[rows:])


def signal_kernel(tok_ref, emission_ref, betas_ref, g_ref, held_ref, table_ref, in_sem, out_sem):
    uniq, states = emission_ref.shape
    rows = betas_ref.shape[0]
    pieces = out_sem.shape[0]
    width = states // pieces
    waits = []
    for piece in range(pieces):
        columns = pl.ds(piece * width, width)
        waits.append(
            (
                start(emission_ref.at[:, columns], table_ref.at[:, columns], in_sem.at[0, piece]),
                start(betas_ref.at[:, columns], held_ref.at[:, columns], in_sem.at[1, piece]),
            )
        )
    tokens = jnp.concatenate([tok_ref[t : t + 1, :] for t in range(tok_ref.shape[0])], axis=1)
    pick = (lax.broadcasted_iota(jnp.int32, (uniq, rows), 0) == tokens).astype(F32).astype(BF16)
    pick = jnp.concatenate([pick, pick, pick], axis=0)
    outs = []
    for piece in range(pieces):
        columns = pl.ds(piece * width, width)
        for copy in waits[piece]:
            copy.wait()
        table = table_ref[:, columns]
        high, rest = split(table)
        middle, low = split(table - high.astype(F32))
        picked = lax.dot_general(
            pick, jnp.concatenate([high, middle, low], axis=0), TN, preferred_element_type=F32
        )
        held_ref[:, columns] = picked * held_ref[:, columns]
        outs.append(start(held_ref.at[:, columns], g_ref.at[:, columns], out_sem.at[piece]))
    for copy in outs:
        copy.wait()


def signal(tokens, emission, betas):
    pieces = 8
    return pl.pallas_call(
        signal_kernel,
        in_specs=[pl.BlockSpec(memory_space=pltpu.VMEM), ANYWHERE, ANYWHERE],
        out_specs=(ANYWHERE, WHOLE),
        out_shape=(pltpu.HBM(betas.shape, F32), jax.ShapeDtypeStruct(betas.shape, F32)),
        scratch_shapes=[
            pltpu.VMEM(emission.shape, F32),
            pltpu.SemaphoreType.DMA((2, pieces)),
            pltpu.SemaphoreType.DMA((pieces,)),
        ],
        compiler_params=pltpu.CompilerParams(vmem_limit_bytes=20 * MIB),
        name="signal",
    )(tokens, emission, betas)


def mixed_kernel(rows_hbm, left_hbm, u_ref, rows_ref, left_ref, sem):
    blocks, _, width = left_ref.shape
    waits = []
    for i in range(blocks):
        columns = pl.ds(i * width, width)
        waits.append(
            (
                start(rows_hbm.at[:, columns], rows_ref.at[i], sem.at[0, i]),
                start(left_hbm.at[i], left_ref.at[i], sem.at[1, i]),
            )
        )
    zs, height, _ = u_ref.shape
    part = height // blocks
    for i in range(blocks):
        for copy in waits[i]:
            copy.wait()
        u = dot3(left_ref[i], rows_ref[i], NT)
        for z in range(zs):
            u_ref[z, i * part : (i + 1) * part, :] = u[z * part : (z + 1) * part]


def mixed(alphas, left, zs):
    rows = alphas.shape[0]
    blocks, window, width = left.shape
    return pl.pallas_call(
        mixed_kernel,
        in_specs=[ANYWHERE, ANYWHERE],
        out_specs=WHOLE,
        out_shape=jax.ShapeDtypeStruct((zs, blocks * window // zs, rows), F32),
        scratch_shapes=[
            pltpu.VMEM((blocks, rows, width), F32),
            pltpu.VMEM(left.shape, F32),
            pltpu.SemaphoreType.DMA((2, blocks)),
        ],
        compiler_params=pltpu.CompilerParams(vmem_limit_bytes=8 * MIB),
        name="mixed",
    )(alphas, left)


def place_of(k):
    return (k // 4 % 2) * 8 + k // 8 * 4 + k % 4


def back_kernel(kcount, ways, place_ref, *refs):
    slots = len(ways)
    rights, refs = (refs[:slots], refs[slots : 2 * slots]), refs[2 * slots :]
    g_ref, u_ref, h_ref, send_ref, right_ref, held_ref = refs
    lanes = u_ref.shape[1]
    chips = slots * slots
    width = g_ref.shape[1] // kcount
    pieces = width // lanes
    krows = 4 * kcount
    rrows = right_ref.shape[1] // chips
    core = place_ref[2]
    for side in range(2):
        owner = core if side == 0 else 1 - core
        on_x = owner == 0
        late = jnp.where(on_x, place_ref[0], place_ref[1])
        early = jnp.where(on_x, place_ref[1], place_ref[0])
        for a, da in enumerate(ways):
            for b, db in enumerate(ways):
                first = lax.rem(late + (slots - da), slots)
                second = lax.rem(early + (slots - db), slots)
                x, y = jnp.where(on_x, first, second), jnp.where(on_x, second, first)
                chip = pl.multiple_of((x * slots + y) * rrows, rrows)
                right_ref[owner, pl.ds(chip, rrows), :] = rights[side][a][b * rrows : (b + 1) * rrows, :]

    part = 2 * kcount
    theirs = pl.multiple_of((1 - core) * part, part)
    for chip in range(chips):
        send_ref[chip * part : (chip + 1) * part, :] = u_ref[pl.ds(chip * 2 * part + theirs, part), :]

    total = jnp.zeros((8, lanes), F32)
    for k in range(kcount):
        r = jnp.concatenate(
            [
                jnp.concatenate(
                    [
                        right_ref[c, pl.ds(k * 2 * pieces + 2 * piece + e, chips, stride=rrows), :]
                        for piece in range(pieces)
                    ],
                    axis=1,
                )
                for c in range(2)
                for e in range(2)
            ],
            axis=0,
        )
        h = dot3(r, g_ref[:, k * width : (k + 1) * width], NT)
        for i in range(4):
            mine = h[i * chips : (i + 1) * chips, :]
            held_ref[pl.ds(i * kcount + place_of(k), chips, stride=krows), :] = mine
            both = u_ref[pl.ds(i * kcount + k, chips, stride=krows), :] * mine
            for top in range(0, chips, 8):
                total = total + both[top : top + 8, :]
    zs, height, _ = h_ref.shape
    body = height - 8
    total = jnp.broadcast_to(jnp.sum(total, axis=0, keepdims=True), total.shape)
    for z in range(zs):
        h_ref[z, 0:body, :] = held_ref[z * body : (z + 1) * body, :]
        h_ref[z, body:height, :] = total


def back(place, ways, rights, others, own, u, zs, kcount):
    rows = own.shape[0]
    body = u.shape[0] // zs
    right = (2, rights[0].shape[0] * len(rights), rights[0].shape[1])
    return pl.pallas_call(
        functools.partial(back_kernel, kcount, ways),
        in_specs=[SCALARS, *[WHOLE for _ in (*rights, *others)], WHOLE, WHOLE],
        out_specs=(WHOLE, WHOLE),
        out_shape=(
            jax.ShapeDtypeStruct((zs, body + 8, rows), F32),
            jax.ShapeDtypeStruct((u.shape[0] // 2, rows), F32),
        ),
        scratch_shapes=[
            pltpu.VMEM(right, F32),
            pltpu.VMEM(u.shape, F32),
        ],
        compiler_params=pltpu.CompilerParams(vmem_limit_bytes=20 * MIB),
        name="back",
    )(place, *rights, *others, own, u)


def gradients_kernel(kcount, scale, place_ref, h_ref, ho_ref, u_ref, uo_ref, *refs):
    rows_refs, g_refs, (out_ref, rows_ref, g_ref, held_ref, rows_sem, g_sem) = refs[:2], refs[2:4], refs[4:]
    blocks, both, width = rows_ref.shape
    lanes = both // 2
    rows_waits, g_waits = [], []
    for i in range(blocks):
        columns = pl.ds(i * width, width)
        rows_waits.append(
            [start(rows_refs[n].at[:, columns], rows_ref.at[i, pl.ds(n * lanes, lanes)], rows_sem.at[n, i]) for n in range(2)]
        )
    steps = g_sem.shape[1]
    share = g_ref.shape[1] // steps
    for step in range(steps):
        columns = pl.ds(step * share, share)
        g_waits.append(
            [start(g_refs[n].at[:, columns], g_ref.at[pl.ds(n * lanes, lanes), columns], g_sem.at[n, step]) for n in range(2)]
        )
    core = place_ref[2]
    chips, out_rows, _ = out_ref.shape
    pieces = width // lanes
    zs = h_ref.shape[0]
    weights = []
    for ref in (h_ref, ho_ref):
        last = ref.shape[1] - 8
        weights.append(scale / sum(ref[z, last : last + 1, :] for z in range(zs)))

    side = round(chips**0.5)
    spots = [jnp.where(core == 0, chip, chip % side * side + chip // side) for chip in range(chips)]
    keep = pl.multiple_of(core * 8, 8)
    for i in range(blocks):
        own = jnp.concatenate([h_ref[z, pl.ds(i * 16 + keep, 8), :] for z in range(zs)], axis=0)
        other = jnp.concatenate([ho_ref[z, pl.ds(i * 16 + keep, 8), :] for z in range(zs)], axis=0)
        h = jnp.concatenate([own * weights[0], other * weights[1]], axis=1)
        for copy in rows_waits[i]:
            copy.wait()
        grad = dot3(h, rows_ref[i], NN)
        depth = grad.shape[0] // chips
        for chip in range(chips):
            for piece in range(pieces):
                first = (i * pieces + piece) * depth
                out_ref[spots[chip], first : first + depth, :] = grad[
                    chip * depth : (chip + 1) * depth, piece * lanes : (piece + 1) * lanes
                ]

    middle = out_rows // 2
    g_width = g_ref.shape[1] // kcount
    g_pieces = g_width // lanes
    for k in range(kcount):
        if k * steps % kcount == 0:
            for copy in g_waits[k * steps // kcount]:
                copy.wait()
        u = jnp.concatenate(
            [
                jnp.concatenate(
                    [
                        u_ref[pl.ds((2 * core + e) * kcount + k, chips, stride=4 * kcount), :] * weights[0],
                        uo_ref[pl.ds(e * kcount + k, chips, stride=2 * kcount), :] * weights[1],
                    ],
                    axis=1,
                )
                for e in range(2)
            ],
            axis=0,
        )
        grad = dot3(u, g_ref[:, k * g_width : (k + 1) * g_width], NN)
        for e in range(2):
            for piece in range(g_pieces):
                place = pl.ds((k * g_pieces + piece) * 2 + e, chips, stride=middle)
                held_ref[place, :] = grad[e * chips : (e + 1) * chips, piece * lanes : (piece + 1) * lanes]
    for chip in range(chips):
        out_ref[spots[chip], middle:, :] = held_ref[chip * middle : (chip + 1) * middle, :]


def gradients(place, h, h_other, u, u_other, alphas, g, chips, kcount, blocks, scale):
    rows, states_in = alphas[0].shape
    states = g[0].shape[1]
    out_rows = (blocks // 2 * (states_in // blocks) * kcount * h.shape[0] + 2 * states * chips) // LANES // chips
    steps = 4
    return pl.pallas_call(
        functools.partial(gradients_kernel, kcount, scale),
        in_specs=[SCALARS] + [WHOLE] * 4 + [ANYWHERE] * 4,
        out_specs=WHOLE,
        out_shape=jax.ShapeDtypeStruct((chips, out_rows, LANES), F32),
        scratch_shapes=[
            pltpu.VMEM((blocks, 2 * rows, states_in // blocks), F32),
            pltpu.VMEM((2 * rows, states), F32),
            pltpu.VMEM((chips * out_rows // 2, LANES), F32),
            pltpu.SemaphoreType.DMA((2, blocks)),
            pltpu.SemaphoreType.DMA((2, steps)),
        ],
        compiler_params=pltpu.CompilerParams(vmem_limit_bytes=20 * MIB),
        name="gradients",
    )(place, h, h_other, u, u_other, *alphas, *g)


def along(stage, core):
    return (stage + core) % 2


def members(nx, ny, stage):
    index = lambda x, y, c: (x * ny + y) * 2 + c
    groups = []
    for c in range(2):
        if along(stage, c) == 0:
            groups += [[index(x, y, c) for x in range(nx)] for y in range(ny)]
        else:
            groups += [[index(x, y, c) for y in range(ny)] for x in range(nx)]
    return groups


def turn(value, groups, distance):
    if distance == 0:
        return value
    pairs = [(line[n], line[(n + distance) % len(line)]) for line in groups for n in range(len(line))]
    return lax.ppermute(value, ("x", "y", "c"), pairs)


def scatter(value, groups):
    parts = lax.all_to_all(
        value, ("x", "y", "c"), split_axis=0, concat_axis=0, axis_index_groups=groups, tiled=True
    )
    n = len(groups[0])
    return jnp.sum(parts.reshape(n, value.shape[0] // n, *value.shape[1:]), axis=0)


def local(alphas, betas, token_ids, emission, left_blocks, right_blocks):
    steps, seq_dev, states_in = alphas.shape
    states_out = betas.shape[2]
    rows = steps * seq_dev
    blocks, window, width = left_blocks.shape
    kcount, rows_right, nblocks = right_blocks.shape
    zs = lax.axis_size("z")
    chips = lax.axis_size("x") * lax.axis_size("y")
    pieces = nblocks // LANES
    scale = window * nblocks / (2.0 * seq_dev * chips * 2)
    swap = functools.partial(lax.ppermute, axis_name="c", perm=[(0, 1), (1, 0)])
    in_hbm = functools.partial(pltpu.with_memory_space_constraint, memory_space=pltpu.HBM)
    place = jnp.stack([lax.axis_index(name) for name in ("x", "y", "c")]).astype(jnp.int32)
    alphas = alphas.reshape(rows, states_in)
    betas = in_hbm(betas.reshape(rows, states_out))

    right_rows = right_blocks.reshape(kcount, rows_right, pieces, LANES).transpose(0, 2, 1, 3)
    right_rows = right_rows.reshape(kcount * pieces * rows_right, LANES)
    side = lax.axis_size("x")
    lines = [members(side, side, stage) for stage in range(2)]
    ways = (0, 1, side - 1) + tuple(range(2, side - 1))
    right_y = jnp.concatenate([turn(right_rows, lines[1], d) for d in ways], axis=0)

    u = mixed(in_hbm(alphas), in_hbm(left_blocks), zs)
    u, right_y = lax.optimization_barrier((u, right_y))
    u = lax.all_to_all(u, "z", split_axis=0, concat_axis=0, tiled=True).reshape(-1, rows)
    rights = [turn(right_y, lines[0], d) for d in ways]
    g_own, g_near = signal(token_ids, in_hbm(emission), betas)
    rights[1], g_own = lax.optimization_barrier((rights[1], g_own))
    others = [swap(part) for part in rights]

    h, u_sent = back(place, ways, rights, others, g_near, u, zs, kcount)
    h, g_later = lax.optimization_barrier((h, g_near))
    h = lax.all_to_all(h, "z", split_axis=0, concat_axis=0, tiled=True)
    h_other, u_other = swap(h), swap(u_sent)

    two_alphas, two_g = (in_hbm(alphas), swap(alphas)), (in_hbm(g_own), swap(g_later))
    part = gradients(place, h, h_other, u, u_other, two_alphas, two_g, chips, kcount, blocks, scale)
    total = scatter(scatter(part, lines[0]), lines[1])[0]
    middle = total.shape[0] // 2
    left_grad = total[:middle].reshape(blocks, pieces, -1, LANES).transpose(0, 2, 1, 3).reshape(blocks, -1, width)
    right_grad = total[middle:].reshape(kcount, pieces, rows_right, LANES).transpose(0, 2, 1, 3)
    return left_grad, right_grad.reshape(kcount, rows_right, nblocks)


def solution(mesh):
    seq, blk = mesh.shape["seq"], mesh.shape["blk"]
    side = round((seq // 2) ** 0.5)
    fine = Mesh(mesh.devices.reshape(side, seq // 2 // side, 2, blk), ("x", "y", "c", "z"))
    s = ("x", "y", "c")
    placed = (
        P(None, s, "z"),
        P(None, s, "z"),
        P(None, s),
        P(None, "z"),
        P("z", None, None),
        P("z", s, None),
    )
    return jax.shard_map(
        local,
        mesh=fine,
        in_specs=placed,
        out_specs=(P("z", s, None), P("z", s, None)),
        check_vma=False,
    )
```

```python
import functools

import jax
import jax.numpy as jnp
from jax import lax
from jax.experimental import pallas as pl
from jax.experimental.pallas import tpu as pltpu
from jax.sharding import Mesh, PartitionSpec as P

F32 = jnp.float32
BF16 = jnp.bfloat16
NT = (((1,), (1,)), ((), ()))
NN = (((1,), (0,)), ((), ()))
TN = (((0,), (0,)), ((), ()))
LANES = 128
MIB = 1024 * 1024
ANYWHERE = pl.BlockSpec(memory_space=pl.ANY)
WHOLE = pl.BlockSpec(memory_space=pltpu.VMEM)
SCALARS = pl.BlockSpec(memory_space=pltpu.SMEM)


def split(value):
    high = value.astype(BF16)
    low = (value - high.astype(F32)).astype(BF16)
    return high, low


def start(source, target, sem):
    copy = pltpu.make_async_copy(source, target, sem)
    copy.start()
    return copy


def dot3(a, b, dims):
    (ah, al), (bh, bl) = split(a), split(b)
    part = functools.partial(lax.dot_general, dimension_numbers=dims, preferred_element_type=F32)
    rows = a.shape[0]
    both = part(jnp.concatenate([ah, al], axis=0), bh)
    return both[:rows] + (part(ah, bl) + both[rows:])


def signal_kernel(tok_ref, emission_ref, betas_ref, g_ref, held_ref, table_ref, in_sem, out_sem):
    uniq, states = emission_ref.shape
    rows = betas_ref.shape[0]
    pieces = out_sem.shape[0]
    width = states // pieces
    waits = []
    for piece in range(pieces):
        columns = pl.ds(piece * width, width)
        waits.append(
            (
                start(emission_ref.at[:, columns], table_ref.at[:, columns], in_sem.at[0, piece]),
                start(betas_ref.at[:, columns], held_ref.at[:, columns], in_sem.at[1, piece]),
            )
        )
    tokens = jnp.concatenate([tok_ref[t : t + 1, :] for t in range(tok_ref.shape[0])], axis=1)
    pick = (lax.broadcasted_iota(jnp.int32, (uniq, rows), 0) == tokens).astype(F32).astype(BF16)
    pick = jnp.concatenate([pick, pick, pick], axis=0)
    outs = []
    for piece in range(pieces):
        columns = pl.ds(piece * width, width)
        for copy in waits[piece]:
            copy.wait()
        table = table_ref[:, columns]
        high, rest = split(table)
        middle, low = split(table - high.astype(F32))
        picked = lax.dot_general(
            pick, jnp.concatenate([high, middle, low], axis=0), TN, preferred_element_type=F32
        )
        held_ref[:, columns] = picked * held_ref[:, columns]
        outs.append(start(held_ref.at[:, columns], g_ref.at[:, columns], out_sem.at[piece]))
    for copy in outs:
        copy.wait()


def signal(tokens, emission, betas):
    pieces = 8
    return pl.pallas_call(
        signal_kernel,
        in_specs=[pl.BlockSpec(memory_space=pltpu.VMEM), ANYWHERE, ANYWHERE],
        out_specs=(ANYWHERE, WHOLE),
        out_shape=(pltpu.HBM(betas.shape, F32), jax.ShapeDtypeStruct(betas.shape, F32)),
        scratch_shapes=[
            pltpu.VMEM(emission.shape, F32),
            pltpu.SemaphoreType.DMA((2, pieces)),
            pltpu.SemaphoreType.DMA((pieces,)),
        ],
        compiler_params=pltpu.CompilerParams(vmem_limit_bytes=20 * MIB),
        name="signal",
    )(tokens, emission, betas)


def mixed_kernel(rows_hbm, left_hbm, u_ref, rows_ref, left_ref, sem):
    blocks, _, width = left_ref.shape
    waits = []
    for i in range(blocks):
        columns = pl.ds(i * width, width)
        waits.append(
            (
                start(rows_hbm.at[:, columns], rows_ref.at[i], sem.at[0, i]),
                start(left_hbm.at[i], left_ref.at[i], sem.at[1, i]),
            )
        )
    zs, height, _ = u_ref.shape
    part = height // blocks
    for i in range(blocks):
        for copy in waits[i]:
            copy.wait()
        u = dot3(left_ref[i], rows_ref[i], NT)
        for z in range(zs):
            u_ref[z, i * part : (i + 1) * part, :] = u[z * part : (z + 1) * part]


def mixed(alphas, left, zs):
    rows = alphas.shape[0]
    blocks, window, width = left.shape
    return pl.pallas_call(
        mixed_kernel,
        in_specs=[ANYWHERE, ANYWHERE],
        out_specs=WHOLE,
        out_shape=jax.ShapeDtypeStruct((zs, blocks * window // zs, rows), F32),
        scratch_shapes=[
            pltpu.VMEM((blocks, rows, width), F32),
            pltpu.VMEM(left.shape, F32),
            pltpu.SemaphoreType.DMA((2, blocks)),
        ],
        compiler_params=pltpu.CompilerParams(vmem_limit_bytes=8 * MIB),
        name="mixed",
    )(alphas, left)


def place_of(k):
    return (k // 4 % 2) * 8 + k // 8 * 4 + k % 4


def back_kernel(kcount, ways, place_ref, *refs):
    slots = len(ways)
    rights, refs = (refs[:slots], refs[slots : 2 * slots]), refs[2 * slots :]
    signal_ref, u_ref, h_ref, send_ref, g_ref, right_ref, held_ref, sem = refs
    lanes = u_ref.shape[1]
    steps = sem.shape[0]
    share = g_ref.shape[1] // steps
    waits = []
    for step in range(steps):
        columns = pl.ds(step * share, share)
        waits.append(start(signal_ref.at[:, columns], g_ref.at[:, columns], sem.at[step]))
    chips = slots * slots
    width = g_ref.shape[1] // kcount
    pieces = width // lanes
    krows = 4 * kcount
    rrows = right_ref.shape[1] // chips
    core = place_ref[2]
    for side in range(2):
        owner = core if side == 0 else 1 - core
        on_x = owner == 0
        late = jnp.where(on_x, place_ref[0], place_ref[1])
        early = jnp.where(on_x, place_ref[1], place_ref[0])
        for a, da in enumerate(ways):
            for b, db in enumerate(ways):
                first = lax.rem(late + (slots - da), slots)
                second = lax.rem(early + (slots - db), slots)
                x, y = jnp.where(on_x, first, second), jnp.where(on_x, second, first)
                chip = pl.multiple_of((x * slots + y) * rrows, rrows)
                right_ref[owner, pl.ds(chip, rrows), :] = rights[side][a][b * rrows : (b + 1) * rrows, :]

    part = 2 * kcount
    theirs = pl.multiple_of((1 - core) * part, part)
    for chip in range(chips):
        send_ref[chip * part : (chip + 1) * part, :] = u_ref[pl.ds(chip * 2 * part + theirs, part), :]

    total = jnp.zeros((8, lanes), F32)
    for k in range(kcount):
        if k * steps % kcount == 0:
            waits[k * steps // kcount].wait()
        r = jnp.concatenate(
            [
                jnp.concatenate(
                    [
                        right_ref[c, pl.ds(k * 2 * pieces + 2 * piece + e, chips, stride=rrows), :]
                        for piece in range(pieces)
                    ],
                    axis=1,
                )
                for c in range(2)
                for e in range(2)
            ],
            axis=0,
        )
        h = dot3(r, g_ref[:, k * width : (k + 1) * width], NT)
        for i in range(4):
            mine = h[i * chips : (i + 1) * chips, :]
            held_ref[pl.ds(i * kcount + place_of(k), chips, stride=krows), :] = mine
            both = u_ref[pl.ds(i * kcount + k, chips, stride=krows), :] * mine
            for top in range(0, chips, 8):
                total = total + both[top : top + 8, :]
    zs, height, _ = h_ref.shape
    body = height - 8
    total = jnp.broadcast_to(jnp.sum(total, axis=0, keepdims=True), total.shape)
    for z in range(zs):
        h_ref[z, 0:body, :] = held_ref[z * body : (z + 1) * body, :]
        h_ref[z, body:height, :] = total


def back(place, ways, rights, others, own, u, zs, kcount):
    rows, states = own.shape
    body = u.shape[0] // zs
    right = (2, rights[0].shape[0] * len(rights), rights[0].shape[1])
    return pl.pallas_call(
        functools.partial(back_kernel, kcount, ways),
        in_specs=[SCALARS, *[WHOLE for _ in (*rights, *others)], ANYWHERE, WHOLE],
        out_specs=(WHOLE, WHOLE),
        out_shape=(
            jax.ShapeDtypeStruct((zs, body + 8, rows), F32),
            jax.ShapeDtypeStruct((u.shape[0] // 2, rows), F32),
        ),
        scratch_shapes=[
            pltpu.VMEM((rows, states), F32),
            pltpu.VMEM(right, F32),
            pltpu.VMEM(u.shape, F32),
            pltpu.SemaphoreType.DMA((4,)),
        ],
        compiler_params=pltpu.CompilerParams(vmem_limit_bytes=20 * MIB),
        name="back",
    )(place, *rights, *others, own, u)


def gradients_kernel(kcount, scale, place_ref, h_ref, ho_ref, u_ref, uo_ref, *refs):
    rows_refs, g_refs, (out_ref, rows_ref, g_ref, held_ref, rows_sem, g_sem) = refs[:2], refs[2:4], refs[4:]
    blocks, both, width = rows_ref.shape
    lanes = both // 2
    rows_waits, g_waits = [], []
    for i in range(blocks):
        columns = pl.ds(i * width, width)
        rows_waits.append(
            [start(rows_refs[n].at[:, columns], rows_ref.at[i, pl.ds(n * lanes, lanes)], rows_sem.at[n, i]) for n in range(2)]
        )
    steps = g_sem.shape[1]
    share = g_ref.shape[1] // steps
    for step in range(steps):
        columns = pl.ds(step * share, share)
        g_waits.append(
            [start(g_refs[n].at[:, columns], g_ref.at[pl.ds(n * lanes, lanes), columns], g_sem.at[n, step]) for n in range(2)]
        )
    core = place_ref[2]
    chips, out_rows, _ = out_ref.shape
    pieces = width // lanes
    zs = h_ref.shape[0]
    weights = []
    for ref in (h_ref, ho_ref):
        last = ref.shape[1] - 8
        weights.append(scale / sum(ref[z, last : last + 1, :] for z in range(zs)))

    side = round(chips**0.5)
    spots = [jnp.where(core == 0, chip, chip % side * side + chip // side) for chip in range(chips)]
    keep = pl.multiple_of(core * 8, 8)
    for i in range(blocks):
        own = jnp.concatenate([h_ref[z, pl.ds(i * 16 + keep, 8), :] for z in range(zs)], axis=0)
        other = jnp.concatenate([ho_ref[z, pl.ds(i * 16 + keep, 8), :] for z in range(zs)], axis=0)
        h = jnp.concatenate([own * weights[0], other * weights[1]], axis=1)
        for copy in rows_waits[i]:
            copy.wait()
        grad = dot3(h, rows_ref[i], NN)
        depth = grad.shape[0] // chips
        for chip in range(chips):
            for piece in range(pieces):
                first = (i * pieces + piece) * depth
                out_ref[spots[chip], first : first + depth, :] = grad[
                    chip * depth : (chip + 1) * depth, piece * lanes : (piece + 1) * lanes
                ]

    middle = out_rows // 2
    g_width = g_ref.shape[1] // kcount
    g_pieces = g_width // lanes
    for k in range(kcount):
        if k * steps % kcount == 0:
            for copy in g_waits[k * steps // kcount]:
                copy.wait()
        u = jnp.concatenate(
            [
                jnp.concatenate(
                    [
                        u_ref[pl.ds((2 * core + e) * kcount + k, chips, stride=4 * kcount), :] * weights[0],
                        uo_ref[pl.ds(e * kcount + k, chips, stride=2 * kcount), :] * weights[1],
                    ],
                    axis=1,
                )
                for e in range(2)
            ],
            axis=0,
        )
        grad = dot3(u, g_ref[:, k * g_width : (k + 1) * g_width], NN)
        for e in range(2):
            for piece in range(g_pieces):
                place = pl.ds((k * g_pieces + piece) * 2 + e, chips, stride=middle)
                held_ref[place, :] = grad[e * chips : (e + 1) * chips, piece * lanes : (piece + 1) * lanes]
    for chip in range(chips):
        out_ref[spots[chip], middle:, :] = held_ref[chip * middle : (chip + 1) * middle, :]


def gradients(place, h, h_other, u, u_other, alphas, g, chips, kcount, blocks, scale):
    rows, states_in = alphas[0].shape
    states = g[0].shape[1]
    out_rows = (blocks // 2 * (states_in // blocks) * kcount * h.shape[0] + 2 * states * chips) // LANES // chips
    steps = 4
    return pl.pallas_call(
        functools.partial(gradients_kernel, kcount, scale),
        in_specs=[SCALARS] + [WHOLE] * 4 + [ANYWHERE] * 4,
        out_specs=WHOLE,
        out_shape=jax.ShapeDtypeStruct((chips, out_rows, LANES), F32),
        scratch_shapes=[
            pltpu.VMEM((blocks, 2 * rows, states_in // blocks), F32),
            pltpu.VMEM((2 * rows, states), F32),
            pltpu.VMEM((chips * out_rows // 2, LANES), F32),
            pltpu.SemaphoreType.DMA((2, blocks)),
            pltpu.SemaphoreType.DMA((2, steps)),
        ],
        compiler_params=pltpu.CompilerParams(vmem_limit_bytes=20 * MIB),
        name="gradients",
    )(place, h, h_other, u, u_other, *alphas, *g)


def along(stage, core):
    return (stage + core) % 2


def members(nx, ny, stage):
    index = lambda x, y, c: (x * ny + y) * 2 + c
    groups = []
    for c in range(2):
        if along(stage, c) == 0:
            groups += [[index(x, y, c) for x in range(nx)] for y in range(ny)]
        else:
            groups += [[index(x, y, c) for y in range(ny)] for x in range(nx)]
    return groups


def turn(value, groups, distance):
    if distance == 0:
        return value
    pairs = [(line[n], line[(n + distance) % len(line)]) for line in groups for n in range(len(line))]
    return lax.ppermute(value, ("x", "y", "c"), pairs)


def scatter(value, groups):
    parts = lax.all_to_all(
        value, ("x", "y", "c"), split_axis=0, concat_axis=0, axis_index_groups=groups, tiled=True
    )
    n = len(groups[0])
    return jnp.sum(parts.reshape(n, value.shape[0] // n, *value.shape[1:]), axis=0)


def local(alphas, betas, token_ids, emission, left_blocks, right_blocks):
    steps, seq_dev, states_in = alphas.shape
    states_out = betas.shape[2]
    rows = steps * seq_dev
    blocks, window, width = left_blocks.shape
    kcount, rows_right, nblocks = right_blocks.shape
    zs = lax.axis_size("z")
    chips = lax.axis_size("x") * lax.axis_size("y")
    pieces = nblocks // LANES
    scale = window * nblocks / (2.0 * seq_dev * chips * 2)
    swap = functools.partial(lax.ppermute, axis_name="c", perm=[(0, 1), (1, 0)])
    in_hbm = functools.partial(pltpu.with_memory_space_constraint, memory_space=pltpu.HBM)
    place = jnp.stack([lax.axis_index(name) for name in ("x", "y", "c")]).astype(jnp.int32)
    alphas = alphas.reshape(rows, states_in)
    betas = in_hbm(betas.reshape(rows, states_out))

    right_rows = right_blocks.reshape(kcount, rows_right, pieces, LANES).transpose(0, 2, 1, 3)
    right_rows = right_rows.reshape(kcount * pieces * rows_right, LANES)
    side = lax.axis_size("x")
    lines = [members(side, side, stage) for stage in range(2)]
    ways = (0, 1, side - 1) + tuple(range(2, side - 1))
    right_y = jnp.concatenate([turn(right_rows, lines[1], d) for d in ways], axis=0)

    u = mixed(in_hbm(alphas), in_hbm(left_blocks), zs)
    u, right_y = lax.optimization_barrier((u, right_y))
    u = lax.all_to_all(u, "z", split_axis=0, concat_axis=0, tiled=True).reshape(-1, rows)
    rights = [turn(right_y, lines[0], d) for d in ways]
    g_own, g_near = signal(token_ids, in_hbm(emission), betas)
    rights[1], g_own = lax.optimization_barrier((rights[1], g_own))
    others = [swap(part) for part in rights]

    h, u_sent = back(place, ways, rights, others, in_hbm(g_own), u, zs, kcount)
    h, g_later = lax.optimization_barrier((h, g_near))
    h = lax.all_to_all(h, "z", split_axis=0, concat_axis=0, tiled=True)
    h_other, u_other = swap(h), swap(u_sent)

    two_alphas, two_g = (in_hbm(alphas), swap(alphas)), (in_hbm(g_own), swap(g_later))
    part = gradients(place, h, h_other, u, u_other, two_alphas, two_g, chips, kcount, blocks, scale)
    total = scatter(scatter(part, lines[0]), lines[1])[0]
    middle = total.shape[0] // 2
    left_grad = total[:middle].reshape(blocks, pieces, -1, LANES).transpose(0, 2, 1, 3).reshape(blocks, -1, width)
    right_grad = total[middle:].reshape(kcount, pieces, rows_right, LANES).transpose(0, 2, 1, 3)
    return left_grad, right_grad.reshape(kcount, rows_right, nblocks)


def solution(mesh):
    seq, blk = mesh.shape["seq"], mesh.shape["blk"]
    side = round((seq // 2) ** 0.5)
    fine = Mesh(mesh.devices.reshape(side, seq // 2 // side, 2, blk), ("x", "y", "c", "z"))
    s = ("x", "y", "c")
    placed = (
        P(None, s, "z"),
        P(None, s, "z"),
        P(None, s),
        P(None, "z"),
        P("z", None, None),
        P("z", s, None),
    )
    return jax.shard_map(
        local,
        mesh=fine,
        in_specs=placed,
        out_specs=(P("z", s, None), P("z", s, None)),
        check_vma=False,
    )
```
